32 devices in a mesh: section: 4 (over z), dp: 4 (over y, x), mp: 2 (over core).
Axes of the slice: x: 2, y: 2, z: 4, core: 2. Of those that a mesh axis runs over, the one named last changes fastest.
Arguments:
- held: bfloat16 [4, 4, 228, 12288], P('section', None, 'dp', 'mp'), may hold values from -6 to 6
- evict_map: int32 [4, 896, 1], P('section', 'dp'), may hold values from 0 to 3; in each aligned block of 224 rows (0 to 223, 224 to 447, ..., all dimensions but the last counted through in order) at most 57 rows name the same one
- cotangent: bfloat16 [4, 896, 12288], P('section', 'dp', 'mp'), may hold values from -6 to 6
- gain: float32 [4, 12288], P('section', 'mp'), may hold values from 0.25 to 1.75
Outputs:
- layer_input_gradient: bfloat16 [4, 896, 12288], P('section', 'dp', 'mp')
- grad_gain: float32 [4, 12288], P('section', 'mp')
The draws below stay inside these ranges and needn't reach their ends.
Inputs may be any that keep to these rules, and one draw needn't show every extreme that they name: `evict_map`: in the tokens of one owner section and replica no holder is named by more than 57 tokens, a bound that some block reaches.
All inputs are finite; a program needn't handle non-finite values.
Results may differ from the reference program's by a relative error of at most 0.0004.
Values may be sent and summed in bfloat16 or wider, within the bound.
A program may use at most 64 MiB of HBM per device.

```python
import math
import jax
import jax.numpy as jnp
import numpy as np
from jax import lax

MODEL_WIDTH = 12288
ROWS = 224
SECTIONS = 4
CAP = 57
N_DP = 4


def levels(key, extent, shards, smallest, largest):
    level = 1.0
    for dim, parts in shards:
        steps = jax.random.uniform(jax.random.fold_in(jax.random.fold_in(key, 6), dim), (parts,), jnp.float32, smallest / len(shards), largest / len(shards))
        level = level * jnp.repeat(jnp.exp(steps), extent[dim] // parts).reshape((-1,) + (1,) * (len(extent) - 1 - dim))
    return level


def assign_block(key, own, number, rows, count, top, reach, slope):
    order = jax.random.permutation(key, count)
    packed, common = shares(count, rows * top, reach, slope, True), shares(count, rows * top, reach, slope, False)
    places = jnp.arange(count)

    def named(sizes, rotation):
        used = int((sizes > 0).sum())
        fixed = max(1, used // 4)
        moved = fixed + (places - fixed + rotation * (used - fixed)) % max(1, count - fixed)
        return jnp.zeros((count,), jnp.int32).at[order[jnp.where(places < fixed, places, moved)]].set(jnp.asarray(sizes, jnp.int32))

    sizes = jnp.where(number % 4 == 0, named(packed, number // 4), named(common, number - number // 4 - 1))
    mixed = jax.random.permutation(jax.random.fold_in(own, 3), count)
    giver, sink = mixed[0:count // 2 * 2:2], mixed[1:count // 2 * 2:2]
    margin = jnp.minimum(sizes[giver] - 1, reach - sizes[sink]) // 2
    margin = jnp.where((giver == order[0]) | (sink == order[0]) | (sizes[sink] == 0), 0, jnp.maximum(margin, 0))
    moved = jax.random.randint(jax.random.fold_in(own, 4), (count // 2,), 0, 1 << 20) % (margin + 1)
    sizes = sizes.at[giver].add(-moved).at[sink].add(moved)
    items = jnp.searchsorted(jnp.cumsum(sizes), jnp.arange(rows * top), side="right").astype(jnp.int32)
    grid = items.reshape(top, rows).T
    grid = grid[jax.random.permutation(jax.random.fold_in(own, 1), rows)]
    rotation = jax.random.randint(jax.random.fold_in(own, 2), (rows, 1), 0, top)
    return jnp.take_along_axis(grid, (jnp.arange(top)[None, :] + rotation) % top, axis=1)


def shares(number_of, total, limit, lean, full):
    loads = [(1 << 20) // math.isqrt(grade ** lean) + 1 for grade in range(1, number_of + 1)]
    largest = limit if full else min(limit, max(-(-total // number_of), total * loads[0] // sum(loads)))
    least = 1 if total - largest >= number_of - 1 else 0
    counts, rest = [largest] + [least] * (number_of - 1), total - largest - least * (number_of - 1)
    while rest > 0:
        movable = [i for i in range(1, number_of) if counts[i] < largest] or [i for i in range(1, number_of) if counts[i] < limit]
        mass, remaining = sum([loads[i] for i in movable]), rest
        for i in movable:
            extra = min(limit - counts[i], max(1, remaining * loads[i] // mass), rest)
            counts[i] = counts[i] + extra
            rest = rest - extra
    return np.array(counts)


def scatter_about(key, shape, scale, most, split=(), kind=jnp.bfloat16):
    array = jax.random.normal(key, shape, jnp.float32) * scale
    if len(split) > 0:
        array = levels(key, shape, split, -0.22, 0.18) * array
    return jnp.clip(array, min=-most, max=most).astype(kind)


def setup_inputs(seed: int = 0) -> dict:
    seeds = jax.random.split(jax.random.key(seed), 5)
    held = scatter_about(seeds[0], (SECTIONS, SECTIONS, N_DP * CAP, MODEL_WIDTH), 1.0, 6.0, ((0, 4), (2, 4), (3, 2)))
    evict_map_keys = jax.random.split(jax.random.fold_in(seeds[1], 1), SECTIONS * (N_DP * ROWS) // ROWS)
    evict_map_turns = jax.random.permutation(jax.random.fold_in(seeds[1], 3), SECTIONS * (N_DP * ROWS) // ROWS)
    evict_map = jax.vmap(lambda own, number: assign_block(jax.random.fold_in(seeds[1], 2), own, number, ROWS, SECTIONS, 1, CAP, 1))(evict_map_keys, evict_map_turns).reshape((SECTIONS, N_DP * ROWS, 1))
    cotangent = scatter_about(seeds[2], (SECTIONS, N_DP * ROWS, MODEL_WIDTH), 1.0, 6.0, ((0, 4), (1, 4), (2, 2)))
    gain = jnp.clip(1.0 + 0.15 * jax.random.normal(seeds[3], (SECTIONS, MODEL_WIDTH), jnp.float32), 0.25, 1.75)
    return {"held": held, "evict_map": evict_map, "cotangent": cotangent, "gain": gain}


def reference(held, evict_map, cotangent, gain):
    sections = held.shape[0]
    hmap = evict_map[:, :, 0].reshape(sections, N_DP, ROWS)
    onehot = (hmap[..., None] == jnp.arange(sections, dtype=jnp.int32)).astype(jnp.int32)
    slots = lax.optimization_barrier(jnp.sum(jnp.cumsum(onehot, axis=2) * onehot, axis=-1)) - 1
    replica = jnp.arange(N_DP, dtype=jnp.int32)[:, None]

    def one_section(index):
        holders = hmap[index]
        places = (replica * CAP + slots[index]).astype(jnp.int32)
        saved_input = held[holders, index, places].reshape(N_DP * ROWS, MODEL_WIDTH).astype(jnp.float32)
        first = lax.optimization_barrier(jnp.sum(saved_input, axis=1, keepdims=True))
        second = lax.optimization_barrier(jnp.sum(saved_input * saved_input, axis=1, keepdims=True))
        row_mean = first / MODEL_WIDTH
        inverse_deviation = 1.0 / jnp.sqrt(second / MODEL_WIDTH - row_mean * row_mean + 1e-05)
        normalized_input = (saved_input - row_mean) * inverse_deviation
        output_gradient = cotangent[index].astype(jnp.float32)
        gain_scaled_gradient = gain[index] * output_gradient
        first_gradient_mean = lax.optimization_barrier(jnp.sum(gain_scaled_gradient, axis=1, keepdims=True)) / MODEL_WIDTH
        second_gradient_mean = lax.optimization_barrier(jnp.sum(gain_scaled_gradient * normalized_input, axis=1, keepdims=True)) / MODEL_WIDTH
        input_gradient_rows = (inverse_deviation * (gain_scaled_gradient - first_gradient_mean - normalized_input * second_gradient_mean)).astype(jnp.bfloat16)
        gain_gradient = lax.optimization_barrier(jnp.sum(output_gradient * normalized_input, axis=0))
        return (input_gradient_rows, gain_gradient)
    layer_input_gradient, grad_gain = lax.map(one_section, jnp.arange(sections, dtype=jnp.int32))
    return (layer_input_gradient, grad_gain)
```

```python
import functools

import jax
import jax.numpy as jnp
from jax import lax
from jax.experimental import pallas as pl
from jax.experimental.pallas import tpu as pltpu
from jax.sharding import PartitionSpec as P

MODEL_WIDTH = 12288
LANES = 128
BLOCK = 32
MESH = pl.DeviceIdType.MESH


def kernel(
    chunk, held, holders, cot_hbm, gain, dx_hbm, gg_out,
    recv, cot, xf, dx, place, part, stats, coef, gsum, gpart,
    send_sem, recv_sem, own_sem, cot_sem, mp_send, mp_recv, dp_send, dp_recv, out_sem,
):
    sections, slots, width = recv.shape
    rows = cot.shape[0]
    chunks = width // chunk
    blocks = rows // BLOCK
    tiles = chunk // LANES
    n_mp, n_dp = stats.shape[0], gpart.shape[0]
    me = lax.axis_index("section")
    my_mp = lax.axis_index("mp")
    my_dp = lax.axis_index("dp")

    barrier = pltpu.get_barrier_semaphore()
    for axis, mine, size in (("section", me, sections), ("mp", my_mp, n_mp), ("dp", my_dp, n_dp)):
        def greet(i, _, axis=axis, mine=mine, size=size):
            pl.semaphore_signal(
                barrier, inc=1, device_id={axis: lax.rem(mine + i, size)}, device_id_type=MESH
            )
            return 0
        lax.fori_loop(1, size, greet, 0)
    own_copy = pltpu.make_async_copy(held.at[0, me], recv.at[me], own_sem)
    cot_copy = pltpu.make_async_copy(cot_hbm.at[0], cot, cot_sem)
    pl.semaphore_wait(barrier, sections + n_mp + n_dp - 3)

    def columns(c):
        return pl.ds(pl.multiple_of(c * chunk, chunk), chunk)

    def outgoing(c, i):
        other = lax.rem(me + i, sections)
        return pltpu.make_async_remote_copy(
            src_ref=held.at[0, other, :, columns(c)],
            dst_ref=recv.at[me, :, columns(c)],
            send_sem=send_sem.at[c, i],
            recv_sem=recv_sem.at[c, me],
            device_id={"section": other},
            device_id_type=MESH,
        )

    def incoming(c, i):
        other = lax.rem(me + i, sections)
        return pltpu.make_async_remote_copy(
            src_ref=held.at[0, other, :, columns(c)],
            dst_ref=recv.at[other, :, columns(c)],
            send_sem=send_sem.at[c, i],
            recv_sem=recv_sem.at[c, other],
            device_id={"section": other},
            device_id_type=MESH,
        )

    def send(c, _):
        def one(i, _):
            outgoing(c, i).start()
            return 0
        return lax.fori_loop(1, sections, one, 0)
    lax.fori_loop(0, chunks, send, 0)
    own_copy.start()
    cot_copy.start()

    holder = holders[0]
    lane = lax.broadcasted_iota(jnp.int32, (rows, LANES), 1)
    onehot = jnp.where(holder == lane, 1.0, 0.0)
    upto = jnp.where(
        lax.broadcasted_iota(jnp.int32, (rows, rows), 0)
        >= lax.broadcasted_iota(jnp.int32, (rows, rows), 1),
        1.0, 0.0,
    ).astype(jnp.bfloat16)
    count = jnp.dot(upto, onehot.astype(jnp.bfloat16), preferred_element_type=jnp.float32)
    slot = jnp.sum(count * onehot, axis=1, keepdims=True) - 1.0
    key = holder.astype(jnp.float32) * slots + slot
    number = lax.broadcasted_iota(jnp.int32, (rows, slots), 1).astype(jnp.float32)
    for s in range(sections):
        place[s] = jnp.where(key == number + float(s * slots), 1.0, 0.0).astype(jnp.bfloat16)
    part[...] = jnp.zeros_like(part)
    gsum[...] = jnp.zeros_like(gsum)

    own_copy.wait()
    cot_copy.wait()

    def work(c, _):
        def arrive(i, _):
            incoming(c, i).wait_recv()
            return 0
        lax.fori_loop(1, sections, arrive, 0)
        cols = columns(c)
        total = jnp.dot(place[0], recv[0, :, cols], preferred_element_type=jnp.float32)
        for s in range(1, sections):
            total += jnp.dot(place[s], recv[s, :, cols], preferred_element_type=jnp.float32)
        xf[:, cols] = total

        def block(b, _):
            rws = pl.ds(pl.multiple_of(b * BLOCK, BLOCK), BLOCK)
            sums = [part[k, rws] for k in range(4)]
            for t in range(tiles):
                at = pl.ds(pl.multiple_of(c * chunk + t * LANES, LANES), LANES)
                x = xf[rws, at]
                g = gain[:, at] * cot[rws, at].astype(jnp.float32)
                sums = [sums[0] + x, sums[1] + x * x, sums[2] + g, sums[3] + g * x]
            for k in range(4):
                part[k, rws] = sums[k]
            return 0
        lax.fori_loop(0, blocks, block, 0)
        return 0
    lax.fori_loop(0, chunks, work, 0)

    lane = lax.broadcasted_iota(jnp.int32, (rows, LANES), 1)
    packed = jnp.zeros((rows, LANES), jnp.float32)
    for k in range(4):
        packed = jnp.where(lane == k, jnp.sum(part[k], axis=1, keepdims=True), packed)
    stats[my_mp] = packed

    def exchange(ref, axis, mine, size, sends, recvs, arriving):
        def copy(i):
            other = lax.rem(mine + i, size)
            return pltpu.make_async_remote_copy(
                src_ref=ref.at[mine],
                dst_ref=ref.at[other if arriving else mine],
                send_sem=sends.at[i],
                recv_sem=recvs.at[other if arriving else mine],
                device_id={axis: other},
                device_id_type=MESH,
            )
        return copy

    mp_out = exchange(stats, "mp", my_mp, n_mp, mp_send, mp_recv, False)
    mp_in = exchange(stats, "mp", my_mp, n_mp, mp_send, mp_recv, True)
    dp_out = exchange(gpart, "dp", my_dp, n_dp, dp_send, dp_recv, False)
    dp_in = exchange(gpart, "dp", my_dp, n_dp, dp_send, dp_recv, True)
    for i in range(1, n_mp):
        mp_out(i).start()
    for i in range(1, n_mp):
        mp_in(i).wait_recv()

    both = stats[0]
    for i in range(1, n_mp):
        both += stats[i]
    mean = both[:, 0:1] / MODEL_WIDTH
    rstd = 1.0 / jnp.sqrt(both[:, 1:2] / MODEL_WIDTH - mean * mean + 1e-05)
    m1 = both[:, 2:3] / MODEL_WIDTH
    m2 = rstd * (both[:, 3:4] / MODEL_WIDTH - mean * m1)
    for k, value in enumerate((mean, rstd, -rstd * rstd * m2, -rstd * m1)):
        coef[k] = jnp.broadcast_to(value, (rows, LANES))

    def gain_block(b, _):
        rws = pl.ds(pl.multiple_of(b * BLOCK, BLOCK), BLOCK)
        mean, rstd = coef[0, rws], coef[1, rws]

        def tile(t, _):
            at = pl.ds(pl.multiple_of(t * LANES, LANES), LANES)
            p = cot[rws, at].astype(jnp.float32) * ((xf[rws, at] - mean) * rstd)
            q = p[0:8]
            for j in range(8, BLOCK, 8):
                q += p[j:j + 8]
            gsum[:, at] += q
            return 0
        return lax.fori_loop(0, width // LANES, tile, 0, unroll=8)
    lax.fori_loop(0, blocks, gain_block, 0)
    gpart[my_dp] = jnp.sum(gsum[...], axis=0, keepdims=True)
    for i in range(1, n_dp):
        dp_out(i).start()

    def out_copy(b):
        rws = pl.ds(pl.multiple_of(b * BLOCK, BLOCK), BLOCK)
        return pltpu.make_async_copy(dx.at[rws], dx_hbm.at[0, rws], out_sem.at[b])

    def grad_block(b, _):
        rws = pl.ds(pl.multiple_of(b * BLOCK, BLOCK), BLOCK)
        mean, rstd, slope, shift = (coef[k, rws] for k in range(4))

        def tile(t, _):
            at = pl.ds(pl.multiple_of(t * LANES, LANES), LANES)
            g = gain[:, at] * cot[rws, at].astype(jnp.float32)
            dx[rws, at] = (rstd * g + shift + (xf[rws, at] - mean) * slope).astype(jnp.bfloat16)
            return 0
        lax.fori_loop(0, width // LANES, tile, 0, unroll=8)
        out_copy(b).start()
        return 0
    lax.fori_loop(0, blocks, grad_block, 0)

    for i in range(1, n_dp):
        dp_in(i).wait_recv()
    total = gpart[0]
    for i in range(1, n_dp):
        total += gpart[i]
    gg_out[...] = total

    def finish(b, _):
        out_copy(b).wait()
        return 0
    lax.fori_loop(0, blocks, finish, 0)
    for i in range(1, n_dp):
        dp_out(i).wait_send()
    for i in range(1, n_mp):
        mp_out(i).wait_send()

    def sent(c, _):
        def one(i, _):
            outgoing(c, i).wait_send()
            return 0
        return lax.fori_loop(1, sections, one, 0)
    lax.fori_loop(0, chunks, sent, 0)


def local(held, evict_map, cotangent, gain):
    sections, n_mp, n_dp = (lax.axis_size(a) for a in ("section", "mp", "dp"))
    _, _, slots, width = held.shape
    rows = cotangent.shape[1]
    chunk = 1024 if width % 1024 == 0 else width
    chunks = width // chunk
    anywhere = pl.BlockSpec(memory_space=pl.ANY)
    vmem = pl.BlockSpec(memory_space=pltpu.VMEM)
    dma = pltpu.SemaphoreType.DMA
    return pl.pallas_call(
        functools.partial(kernel, chunk),
        out_shape=(
            jax.ShapeDtypeStruct((1, rows, width), jnp.bfloat16),
            jax.ShapeDtypeStruct((1, width), jnp.float32),
        ),
        in_specs=[anywhere, vmem, anywhere, vmem],
        out_specs=(anywhere, vmem),
        scratch_shapes=[
            pltpu.VMEM((sections, slots, width), jnp.bfloat16),
            pltpu.VMEM((rows, width), jnp.bfloat16),
            pltpu.VMEM((rows, width), jnp.float32),
            pltpu.VMEM((rows, width), jnp.bfloat16),
            pltpu.VMEM((sections, rows, slots), jnp.bfloat16),
            pltpu.VMEM((4, rows, LANES), jnp.float32),
            pltpu.VMEM((n_mp, rows, LANES), jnp.float32),
            pltpu.VMEM((4, rows, LANES), jnp.float32),
            pltpu.VMEM((8, width), jnp.float32),
            pltpu.VMEM((n_dp, 1, width), jnp.float32),
            dma((chunks, sections)),
            dma((chunks, sections)),
            dma(()),
            dma(()),
            dma((n_mp,)),
            dma((n_mp,)),
            dma((n_dp,)),
            dma((n_dp,)),
            dma((rows // BLOCK,)),
        ],
        compiler_params=pltpu.CompilerParams(
            collective_id=0, has_side_effects=True, vmem_limit_bytes=48 * 1024 * 1024
        ),
        cost_estimate=pl.CostEstimate(
            flops=2 * rows * sections * slots * width,
            bytes_accessed=2 * width * (sections * slots + 2 * rows),
            transcendentals=0,
        ),
    )(held, evict_map, cotangent, gain)


def solution(mesh):
    placed = (
        P("section", None, "dp", "mp"),
        P("section", "dp", None),
        P("section", "dp", "mp"),
        P("section", "mp"),
    )
    return jax.shard_map(
        local,
        mesh=mesh,
        in_specs=placed,
        out_specs=(P("section", "dp", "mp"), P("section", "mp")),
        check_vma=False,
    )
```

```python
import functools

import jax
import jax.numpy as jnp
from jax import lax
from jax.experimental import pallas as pl
from jax.experimental.pallas import tpu as pltpu
from jax.sharding import PartitionSpec as P

MODEL_WIDTH = 12288
LANES = 128
BLOCK = 32
MESH = pl.DeviceIdType.MESH


def kernel(
    chunk, held, holders_hbm, cot_hbm, gain_hbm, dx_hbm, gg_out,
    mixed, outbox, recv, odd_out, odd_in, holders, gain, cot, xf, dx, place, part, stats, coef, gsum, gpart,
    held_sem, send_sem, recv_sem, odd_held_sem, odd_send, odd_recv, holders_sem, gain_sem, cot_sem,
    mp_send, mp_recv, dp_send, dp_recv, out_sem,
):
    slots, sections, width = held.shape
    padded = recv.shape[1]
    main = min(slots, padded)
    odd = slots - main
    rows = cot.shape[0]
    chunks = width // chunk
    blocks = rows // BLOCK
    tiles = chunk // LANES
    n_mp, n_dp = stats.shape[0], gpart.shape[0]
    me = lax.axis_index("section")
    my_mp = lax.axis_index("mp")
    my_dp = lax.axis_index("dp")

    barrier = pltpu.get_barrier_semaphore()
    for axis, mine, size in (("section", me, sections), ("mp", my_mp, n_mp), ("dp", my_dp, n_dp)):
        def greet(i, _, axis=axis, mine=mine, size=size):
            pl.semaphore_signal(
                barrier, inc=1, device_id={axis: lax.rem(mine + i, size)}, device_id_type=MESH
            )
            return 0
        lax.fori_loop(1, size, greet, 0)

    def columns(c):
        return pl.ds(pl.multiple_of(c * chunk, chunk), chunk)

    def fetch(c):
        return pltpu.make_async_copy(
            held.at[0:main, :, columns(c)], mixed.at[0:main, :, columns(c)], held_sem.at[c]
        )
    def start_fetch(c, _):
        fetch(c).start()
        return 0
    lax.fori_loop(0, chunks, start_fetch, 0)
    if odd:
        odd_fetch = pltpu.make_async_copy(
            held.at[main:slots], mixed.at[main:slots], odd_held_sem
        )
        odd_fetch.start()
    cot_copy = pltpu.make_async_copy(cot_hbm.at[0], cot, cot_sem)
    cot_copy.start()
    holders_copy = pltpu.make_async_copy(holders_hbm, holders, holders_sem)
    holders_copy.start()
    gain_copy = pltpu.make_async_copy(gain_hbm, gain, gain_sem)
    gain_copy.start()

    here = lax.broadcasted_iota(jnp.int32, (padded, main * sections), 0)
    there = lax.broadcasted_iota(jnp.int32, (padded, main * sections), 1)
    by_owner = jnp.concatenate(
        [jnp.where(here * sections + s == there, 1.0, 0.0) for s in range(sections)], axis=0
    ).astype(jnp.bfloat16)

    def outgoing(c, i):
        other = lax.rem(me + i, sections)
        return pltpu.make_async_remote_copy(
            src_ref=outbox.at[other, :, columns(c)],
            dst_ref=recv.at[me, :, columns(c)],
            send_sem=send_sem.at[c, i],
            recv_sem=recv_sem.at[c, me],
            device_id={"section": other},
            device_id_type=MESH,
        )

    def incoming(c, i):
        other = lax.rem(me + i, sections)
        return pltpu.make_async_remote_copy(
            src_ref=outbox.at[other, :, columns(c)],
            dst_ref=recv.at[other, :, columns(c)],
            send_sem=send_sem.at[c, i],
            recv_sem=recv_sem.at[c, other],
            device_id={"section": other},
            device_id_type=MESH,
        )

    def odd_copy(i, arriving):
        other = lax.rem(me + i, sections)
        origin = other if arriving else me
        return pltpu.make_async_remote_copy(
            src_ref=odd_out.at[other],
            dst_ref=odd_in.at[origin],
            send_sem=odd_send.at[i],
            recv_sem=odd_recv.at[origin],
            device_id={"section": other},
            device_id_type=MESH,
        )

    def send(c, _):
        fetch(c).wait()
        cols = columns(c)
        rows_by_slot = mixed[0:main, :, cols].reshape(main * sections, chunk)
        sorted_rows = jnp.dot(
            by_owner, rows_by_slot, preferred_element_type=jnp.float32
        ).astype(jnp.bfloat16)
        for s in range(sections):
            outbox[s, :, cols] = sorted_rows[s * padded:(s + 1) * padded]

        def one(i, _):
            outgoing(c, i).start()
            return 0
        lax.fori_loop(1, sections, one, 0)
        recv[me, :, cols] = outbox[me, :, cols]
        return 0

    pl.semaphore_wait(barrier, sections + n_mp + n_dp - 3)
    send(0, 0)
    if odd:
        odd_fetch.wait()
        for k in range(odd):
            last = mixed[main + k].astype(jnp.float32)
            for s in range(sections):
                odd_out[s, k:k + 1, :] = last[s:s + 1]

        def send_odd(i, _):
            odd_copy(i, False).start()
            return 0
        lax.fori_loop(1, sections, send_odd, 0)
        odd_in[me] = odd_out[me]
    lax.fori_loop(1, chunks, send, 0)

    holders_copy.wait()
    across = lax.broadcasted_iota(jnp.int32, (rows, rows), 1)
    down = lax.broadcasted_iota(jnp.int32, (rows, rows), 0)
    named = holders[...].astype(jnp.float32)
    holder = jnp.sum(jnp.where(across == down, named, 0.0), axis=1, keepdims=True)
    lane = lax.broadcasted_iota(jnp.int32, (rows, LANES), 1)
    onehot = jnp.where(holder == lane.astype(jnp.float32), 1.0, 0.0)
    upto = jnp.where(down >= across, 1.0, 0.0).astype(jnp.bfloat16)
    count = jnp.dot(upto, onehot.astype(jnp.bfloat16), preferred_element_type=jnp.float32)
    slot = jnp.sum(count * onehot, axis=1, keepdims=True) - 1.0
    number = lax.broadcasted_iota(jnp.int32, (rows, padded), 1).astype(jnp.float32)
    for s in range(sections):
        place[s] = jnp.where(
            jnp.logical_and(holder == float(s), slot == number), 1.0, 0.0
        ).astype(jnp.bfloat16)
    number = lax.broadcasted_iota(jnp.int32, (rows, sections), 1).astype(jnp.float32)
    odd_place = [
        jnp.where(
            jnp.logical_and(holder == number, slot == float(main + k)), 1.0, 0.0
        ).astype(jnp.bfloat16)
        for k in range(odd)
    ]
    part[...] = jnp.zeros_like(part)
    gsum[...] = jnp.zeros_like(gsum)

    cot_copy.wait()
    gain_copy.wait()
    if odd:
        def odd_arrive(i, _):
            odd_copy(i, True).wait_recv()
            return 0
        lax.fori_loop(1, sections, odd_arrive, 0)

    def work(c, _):
        def arrive(i, _):
            incoming(c, i).wait_recv()
            return 0
        lax.fori_loop(1, sections, arrive, 0)
        cols = columns(c)
        total = jnp.dot(place[0], recv[0, :, cols], preferred_element_type=jnp.float32)
        for s in range(1, sections):
            total += jnp.dot(place[s], recv[s, :, cols], preferred_element_type=jnp.float32)
        for k in range(odd):
            extra = jnp.concatenate([odd_in[s, k:k + 1, cols] for s in range(sections)], axis=0)
            total += jnp.dot(
                odd_place[k], extra.astype(jnp.bfloat16), preferred_element_type=jnp.float32
            )
        xf[:, cols] = total

        def block(b, _):
            rws = pl.ds(pl.multiple_of(b * BLOCK, BLOCK), BLOCK)
            sums = [part[k, rws] for k in range(4)]
            for t in range(tiles):
                at = pl.ds(pl.multiple_of(c * chunk + t * LANES, LANES), LANES)
                x = xf[rws, at]
                g = gain[:, at] * cot[rws, at].astype(jnp.float32)
                sums = [sums[0] + x, sums[1] + x * x, sums[2] + g, sums[3] + g * x]
            for k in range(4):
                part[k, rws] = sums[k]
            return 0
        lax.fori_loop(0, blocks, block, 0)
        return 0
    lax.fori_loop(0, chunks, work, 0)

    lane = lax.broadcasted_iota(jnp.int32, (rows, LANES), 1)
    packed = jnp.zeros((rows, LANES), jnp.float32)
    for k in range(4):
        packed = jnp.where(lane == k, jnp.sum(part[k], axis=1, keepdims=True), packed)
    stats[my_mp] = packed

    def exchange(ref, axis, mine, size, sends, recvs, arriving):
        def copy(i):
            other = lax.rem(mine + i, size)
            return pltpu.make_async_remote_copy(
                src_ref=ref.at[mine],
                dst_ref=ref.at[other if arriving else mine],
                send_sem=sends.at[i],
                recv_sem=recvs.at[other if arriving else mine],
                device_id={axis: other},
                device_id_type=MESH,
            )
        return copy

    mp_out = exchange(stats, "mp", my_mp, n_mp, mp_send, mp_recv, False)
    mp_in = exchange(stats, "mp", my_mp, n_mp, mp_send, mp_recv, True)
    dp_out = exchange(gpart, "dp", my_dp, n_dp, dp_send, dp_recv, False)
    dp_in = exchange(gpart, "dp", my_dp, n_dp, dp_send, dp_recv, True)
    for i in range(1, n_mp):
        mp_out(i).start()
    for i in range(1, n_mp):
        mp_in(i).wait_recv()

    both = stats[0]
    for i in range(1, n_mp):
        both += stats[i]
    mean = both[:, 0:1] / MODEL_WIDTH
    rstd = 1.0 / jnp.sqrt(both[:, 1:2] / MODEL_WIDTH - mean * mean + 1e-05)
    m1 = both[:, 2:3] / MODEL_WIDTH
    m2 = rstd * (both[:, 3:4] / MODEL_WIDTH - mean * m1)
    for k, value in enumerate((mean, rstd, -rstd * rstd * m2, -rstd * m1)):
        coef[k] = jnp.broadcast_to(value, (rows, LANES))

    def gain_block(b, _):
        rws = pl.ds(pl.multiple_of(b * BLOCK, BLOCK), BLOCK)
        mean, rstd = coef[0, rws], coef[1, rws]

        def tile(t, _):
            at = pl.ds(pl.multiple_of(t * LANES, LANES), LANES)
            p = cot[rws, at].astype(jnp.float32) * ((xf[rws, at] - mean) * rstd)
            q = p[0:8]
            for j in range(8, BLOCK, 8):
                q += p[j:j + 8]
            gsum[:, at] += q
            return 0
        return lax.fori_loop(0, width // LANES, tile, 0, unroll=8)
    lax.fori_loop(0, blocks, gain_block, 0)
    gpart[my_dp] = jnp.sum(gsum[...], axis=0, keepdims=True)
    for i in range(1, n_dp):
        dp_out(i).start()

    def out_copy(b):
        rws = pl.ds(pl.multiple_of(b * BLOCK, BLOCK), BLOCK)
        return pltpu.make_async_copy(dx.at[rws], dx_hbm.at[0, rws], out_sem.at[b])

    def grad_block(b, _):
        rws = pl.ds(pl.multiple_of(b * BLOCK, BLOCK), BLOCK)
        mean, rstd, slope, shift = (coef[k, rws] for k in range(4))

        def tile(t, _):
            at = pl.ds(pl.multiple_of(t * LANES, LANES), LANES)
            g = gain[:, at] * cot[rws, at].astype(jnp.float32)
            dx[rws, at] = (rstd * g + shift + (xf[rws, at] - mean) * slope).astype(jnp.bfloat16)
            return 0
        lax.fori_loop(0, width // LANES, tile, 0, unroll=8)
        out_copy(b).start()
        return 0
    lax.fori_loop(0, blocks, grad_block, 0)

    for i in range(1, n_dp):
        dp_in(i).wait_recv()
    total = gpart[0]
    for i in range(1, n_dp):
        total += gpart[i]
    gg_out[...] = total

    def finish(b, _):
        out_copy(b).wait()
        return 0
    lax.fori_loop(0, blocks, finish, 0)

    for i in range(1, n_dp):
        dp_out(i).wait_send()
    for i in range(1, n_mp):
        mp_out(i).wait_send()

    def sent(c, _):
        def one(i, _):
            outgoing(c, i).wait_send()
            return 0
        return lax.fori_loop(1, sections, one, 0)
    lax.fori_loop(0, chunks, sent, 0)
    if odd:
        def odd_sent(i, _):
            odd_copy(i, False).wait_send()
            return 0
        lax.fori_loop(1, sections, odd_sent, 0)


def local(held, evict_map, cotangent, gain):
    sections, n_mp, n_dp = (lax.axis_size(a) for a in ("section", "mp", "dp"))
    _, _, slots, width = held.shape
    rows = cotangent.shape[1]
    chunk = 512 if width % 512 == 0 else width
    chunks = width // chunk
    odd = slots % 8 if slots > 8 and slots % 8 <= 3 else 0
    padded = -(-(slots - odd) // 8) * 8
    outside = pl.BlockSpec(memory_space=pltpu.HBM)
    vmem = pl.BlockSpec(memory_space=pltpu.VMEM)
    dma = pltpu.SemaphoreType.DMA
    return pl.pallas_call(
        functools.partial(kernel, chunk),
        out_shape=(
            jax.ShapeDtypeStruct((1, rows, width), jnp.bfloat16),
            jax.ShapeDtypeStruct((1, width), jnp.float32),
        ),
        in_specs=[outside] * 4,
        out_specs=(outside, vmem),
        scratch_shapes=[
            pltpu.VMEM((slots, sections, width), jnp.bfloat16),
            pltpu.VMEM((sections, padded, width), jnp.bfloat16),
            pltpu.VMEM((sections, padded, width), jnp.bfloat16),
            pltpu.VMEM((sections, max(odd, 1), width), jnp.float32),
            pltpu.VMEM((sections, max(odd, 1), width), jnp.float32),
            pltpu.VMEM((1, rows), jnp.int32),
            pltpu.VMEM((1, width), jnp.float32),
            pltpu.VMEM((rows, width), jnp.bfloat16),
            pltpu.VMEM((rows, width), jnp.float32),
            pltpu.VMEM((rows, width), jnp.bfloat16),
            pltpu.VMEM((sections, rows, padded), jnp.bfloat16),
            pltpu.VMEM((4, rows, LANES), jnp.float32),
            pltpu.VMEM((n_mp, rows, LANES), jnp.float32),
            pltpu.VMEM((4, rows, LANES), jnp.float32),
            pltpu.VMEM((8, width), jnp.float32),
            pltpu.VMEM((n_dp, 1, width), jnp.float32),
            dma((chunks,)),
            dma((chunks, sections)),
            dma((chunks, sections)),
            dma(()),
            dma((sections,)),
            dma((sections,)),
            dma(()),
            dma(()),
            dma(()),
            dma((n_mp,)),
            dma((n_mp,)),
            dma((n_dp,)),
            dma((n_dp,)),
            dma((rows // BLOCK,)),
        ],
        compiler_params=pltpu.CompilerParams(
            collective_id=0, has_side_effects=True, vmem_limit_bytes=56 * 1024 * 1024
        ),
        cost_estimate=pl.CostEstimate(
            flops=2 * rows * sections * slots * width,
            bytes_accessed=2 * width * (sections * slots + 2 * rows),
            transcendentals=0,
        ),
    )(jnp.transpose(held[0], (1, 0, 2)), evict_map.reshape(1, rows), cotangent, gain)


def solution(mesh):
    placed = (
        P("section", None, "dp", "mp"),
        P("section", "dp", None),
        P("section", "dp", "mp"),
        P("section", "mp"),
    )
    return jax.shard_map(
        local,
        mesh=mesh,
        in_specs=placed,
        out_specs=(P("section", "dp", "mp"), P("section", "mp")),
        check_vma=False,
    )
```

```python
import functools

import jax
import jax.numpy as jnp
from jax import lax
from jax.experimental import pallas as pl
from jax.experimental.pallas import tpu as pltpu
from jax.sharding import PartitionSpec as P

MODEL_WIDTH = 12288
LANES = 128
BLOCK = 32
MESH = pl.DeviceIdType.MESH


def kernel(
    chunk, held, holders_hbm, cot_hbm, gain_hbm, dx, gg_out,
    mixed, outbox, recv, odd_out, odd_in, holders, gain, cot, xf, place, part, stats, coef, gsum, gpart,
    held_sem, send_sem, recv_sem, odd_held_sem, odd_send, odd_recv, holders_sem, gain_sem, cot_sem,
    mp_send, mp_recv, dp_send, dp_recv,
):
    slots, sections, width = held.shape
    padded = recv.shape[1]
    main = min(slots, padded)
    odd = slots - main
    rows = cot.shape[0]
    chunks = width // chunk
    blocks = rows // BLOCK
    tiles = chunk // LANES
    n_mp, n_dp = stats.shape[0], gpart.shape[0]
    me = lax.axis_index("section")
    my_mp = lax.axis_index("mp")
    my_dp = lax.axis_index("dp")

    barrier = pltpu.get_barrier_semaphore()
    for axis, mine, size in (("section", me, sections), ("mp", my_mp, n_mp), ("dp", my_dp, n_dp)):
        def greet(i, _, axis=axis, mine=mine, size=size):
            pl.semaphore_signal(
                barrier, inc=1, device_id={axis: lax.rem(mine + i, size)}, device_id_type=MESH
            )
            return 0
        lax.fori_loop(1, size, greet, 0)

    def columns(c):
        return pl.ds(pl.multiple_of(c * chunk, chunk), chunk)

    def fetch(c):
        return pltpu.make_async_copy(
            held.at[0:main, :, columns(c)], mixed.at[0:main, :, columns(c)], held_sem.at[c]
        )
    def start_fetch(c, _):
        fetch(c).start()
        return 0
    lax.fori_loop(0, chunks, start_fetch, 0)
    if odd:
        odd_fetch = pltpu.make_async_copy(
            held.at[main:slots], mixed.at[main:slots], odd_held_sem
        )
        odd_fetch.start()
    cot_copy = pltpu.make_async_copy(cot_hbm.at[0], cot, cot_sem)
    cot_copy.start()
    holders_copy = pltpu.make_async_copy(holders_hbm, holders, holders_sem)
    holders_copy.start()
    gain_copy = pltpu.make_async_copy(gain_hbm, gain, gain_sem)
    gain_copy.start()

    here = lax.broadcasted_iota(jnp.int32, (padded, main * sections), 0)
    there = lax.broadcasted_iota(jnp.int32, (padded, main * sections), 1)
    by_owner = jnp.concatenate(
        [jnp.where(here * sections + s == there, 1.0, 0.0) for s in range(sections)], axis=0
    ).astype(jnp.bfloat16)

    def outgoing(c, i):
        other = lax.rem(me + i, sections)
        return pltpu.make_async_remote_copy(
            src_ref=outbox.at[other, :, columns(c)],
            dst_ref=recv.at[me, :, columns(c)],
            send_sem=send_sem.at[c, i],
            recv_sem=recv_sem.at[c, me],
            device_id={"section": other},
            device_id_type=MESH,
        )

    def incoming(c, i):
        other = lax.rem(me + i, sections)
        return pltpu.make_async_remote_copy(
            src_ref=outbox.at[other, :, columns(c)],
            dst_ref=recv.at[other, :, columns(c)],
            send_sem=send_sem.at[c, i],
            recv_sem=recv_sem.at[c, other],
            device_id={"section": other},
            device_id_type=MESH,
        )

    def odd_copy(i, arriving):
        other = lax.rem(me + i, sections)
        origin = other if arriving else me
        return pltpu.make_async_remote_copy(
            src_ref=odd_out.at[other],
            dst_ref=odd_in.at[origin],
            send_sem=odd_send.at[i],
            recv_sem=odd_recv.at[origin],
            device_id={"section": other},
            device_id_type=MESH,
        )

    def send(c, _):
        fetch(c).wait()
        cols = columns(c)
        rows_by_slot = mixed[0:main, :, cols].reshape(main * sections, chunk)
        sorted_rows = jnp.dot(
            by_owner, rows_by_slot, preferred_element_type=jnp.float32
        ).astype(jnp.bfloat16)
        for s in range(sections):
            outbox[s, :, cols] = sorted_rows[s * padded:(s + 1) * padded]

        def one(i, _):
            outgoing(c, i).start()
            return 0
        lax.fori_loop(1, sections, one, 0)
        recv[me, :, cols] = outbox[me, :, cols]
        return 0

    pl.semaphore_wait(barrier, sections + n_mp + n_dp - 3)
    send(0, 0)
    if odd:
        odd_fetch.wait()
        for k in range(odd):
            last = mixed[main + k].astype(jnp.float32)
            for s in range(sections):
                odd_out[s, k:k + 1, :] = last[s:s + 1]

        def send_odd(i, _):
            odd_copy(i, False).start()
            return 0
        lax.fori_loop(1, sections, send_odd, 0)
        odd_in[me] = odd_out[me]
    lax.fori_loop(1, chunks, send, 0)

    holders_copy.wait()
    across = lax.broadcasted_iota(jnp.int32, (rows, rows), 1)
    down = lax.broadcasted_iota(jnp.int32, (rows, rows), 0)
    named = holders[...].astype(jnp.float32)
    holder = jnp.sum(jnp.where(across == down, named, 0.0), axis=1, keepdims=True)
    lane = lax.broadcasted_iota(jnp.int32, (rows, LANES), 1)
    onehot = jnp.where(holder == lane.astype(jnp.float32), 1.0, 0.0)
    upto = jnp.where(down >= across, 1.0, 0.0).astype(jnp.bfloat16)
    count = jnp.dot(upto, onehot.astype(jnp.bfloat16), preferred_element_type=jnp.float32)
    slot = jnp.sum(count * onehot, axis=1, keepdims=True) - 1.0
    number = lax.broadcasted_iota(jnp.int32, (rows, padded), 1).astype(jnp.float32)
    for s in range(sections):
        place[s] = jnp.where(
            jnp.logical_and(holder == float(s), slot == number), 1.0, 0.0
        ).astype(jnp.bfloat16)
    number = lax.broadcasted_iota(jnp.int32, (rows, sections), 1).astype(jnp.float32)
    odd_place = [
        jnp.where(
            jnp.logical_and(holder == number, slot == float(main + k)), 1.0, 0.0
        ).astype(jnp.bfloat16)
        for k in range(odd)
    ]
    part[...] = jnp.zeros_like(part)
    gsum[...] = jnp.zeros_like(gsum)

    cot_copy.wait()
    gain_copy.wait()
    if odd:
        def odd_arrive(i, _):
            odd_copy(i, True).wait_recv()
            return 0
        lax.fori_loop(1, sections, odd_arrive, 0)

    def work(c, _):
        def arrive(i, _):
            incoming(c, i).wait_recv()
            return 0
        lax.fori_loop(1, sections, arrive, 0)
        cols = columns(c)
        total = jnp.dot(place[0], recv[0, :, cols], preferred_element_type=jnp.float32)
        for s in range(1, sections):
            total += jnp.dot(place[s], recv[s, :, cols], preferred_element_type=jnp.float32)
        for k in range(odd):
            extra = jnp.concatenate([odd_in[s, k:k + 1, cols] for s in range(sections)], axis=0)
            total += jnp.dot(
                odd_place[k], extra.astype(jnp.bfloat16), preferred_element_type=jnp.float32
            )
        xf[:, cols] = total

        def block(b, _):
            rws = pl.ds(pl.multiple_of(b * BLOCK, BLOCK), BLOCK)
            sums = [part[k, rws] for k in range(4)]
            for t in range(tiles):
                at = pl.ds(pl.multiple_of(c * chunk + t * LANES, LANES), LANES)
                x = xf[rws, at]
                g = gain[:, at] * cot[rws, at].astype(jnp.float32)
                sums = [sums[0] + x, sums[1] + x * x, sums[2] + g, sums[3] + g * x]
            for k in range(4):
                part[k, rws] = sums[k]
            return 0
        lax.fori_loop(0, blocks, block, 0)
        return 0
    lax.fori_loop(0, chunks, work, 0)

    lane = lax.broadcasted_iota(jnp.int32, (rows, LANES), 1)
    packed = jnp.zeros((rows, LANES), jnp.float32)
    for k in range(4):
        packed = jnp.where(lane == k, jnp.sum(part[k], axis=1, keepdims=True), packed)
    stats[my_mp] = packed

    def exchange(ref, axis, mine, size, sends, recvs, arriving):
        def copy(i):
            other = lax.rem(mine + i, size)
            return pltpu.make_async_remote_copy(
                src_ref=ref.at[mine],
                dst_ref=ref.at[other if arriving else mine],
                send_sem=sends.at[i],
                recv_sem=recvs.at[other if arriving else mine],
                device_id={axis: other},
                device_id_type=MESH,
            )
        return copy

    mp_out = exchange(stats, "mp", my_mp, n_mp, mp_send, mp_recv, False)
    mp_in = exchange(stats, "mp", my_mp, n_mp, mp_send, mp_recv, True)
    dp_out = exchange(gpart, "dp", my_dp, n_dp, dp_send, dp_recv, False)
    dp_in = exchange(gpart, "dp", my_dp, n_dp, dp_send, dp_recv, True)
    for i in range(1, n_mp):
        mp_out(i).start()
    for i in range(1, n_mp):
        mp_in(i).wait_recv()

    both = stats[0]
    for i in range(1, n_mp):
        both += stats[i]
    mean = both[:, 0:1] / MODEL_WIDTH
    rstd = 1.0 / jnp.sqrt(both[:, 1:2] / MODEL_WIDTH - mean * mean + 1e-05)
    m1 = both[:, 2:3] / MODEL_WIDTH
    m2 = rstd * (both[:, 3:4] / MODEL_WIDTH - mean * m1)
    for k, value in enumerate((mean, rstd, -rstd * rstd * m2, -rstd * m1)):
        coef[k] = jnp.broadcast_to(value, (rows, LANES))

    def gain_block(b, _):
        rws = pl.ds(pl.multiple_of(b * BLOCK, BLOCK), BLOCK)
        mean, rstd = coef[0, rws], coef[1, rws]

        def tile(t, _):
            at = pl.ds(pl.multiple_of(t * LANES, LANES), LANES)
            p = cot[rws, at].astype(jnp.float32) * ((xf[rws, at] - mean) * rstd)
            q = p[0:8]
            for j in range(8, BLOCK, 8):
                q += p[j:j + 8]
            gsum[:, at] += q
            return 0
        return lax.fori_loop(0, width // LANES, tile, 0, unroll=8)
    lax.fori_loop(0, blocks, gain_block, 0)
    gpart[my_dp] = jnp.sum(gsum[...], axis=0, keepdims=True)
    for i in range(1, n_dp):
        dp_out(i).start()

    def grad_block(b, _):
        rws = pl.ds(pl.multiple_of(b * BLOCK, BLOCK), BLOCK)
        mean, rstd, slope, shift = (coef[k, rws] for k in range(4))

        def tile(t, _):
            at = pl.ds(pl.multiple_of(t * LANES, LANES), LANES)
            g = gain[:, at] * cot[rws, at].astype(jnp.float32)
            dx[0, rws, at] = (rstd * g + shift + (xf[rws, at] - mean) * slope).astype(jnp.bfloat16)
            return 0
        lax.fori_loop(0, width // LANES, tile, 0, unroll=8)
        return 0
    lax.fori_loop(0, blocks, grad_block, 0)

    for i in range(1, n_dp):
        dp_in(i).wait_recv()
    total = gpart[0]
    for i in range(1, n_dp):
        total += gpart[i]
    gg_out[...] = total

    for i in range(1, n_dp):
        dp_out(i).wait_send()
    for i in range(1, n_mp):
        mp_out(i).wait_send()

    def sent(c, _):
        def one(i, _):
            outgoing(c, i).wait_send()
            return 0
        return lax.fori_loop(1, sections, one, 0)
    lax.fori_loop(0, chunks, sent, 0)
    if odd:
        def odd_sent(i, _):
            odd_copy(i, False).wait_send()
            return 0
        lax.fori_loop(1, sections, odd_sent, 0)


def local(held, evict_map, cotangent, gain):
    sections, n_mp, n_dp = (lax.axis_size(a) for a in ("section", "mp", "dp"))
    _, _, slots, width = held.shape
    rows = cotangent.shape[1]
    chunk = 512 if width % 512 == 0 else width
    chunks = width // chunk
    odd = slots % 8 if slots > 8 and slots % 8 <= 3 else 0
    padded = -(-(slots - odd) // 8) * 8
    outside = pl.BlockSpec(memory_space=pltpu.HBM)
    vmem = pl.BlockSpec(memory_space=pltpu.VMEM)
    dma = pltpu.SemaphoreType.DMA
    return pl.pallas_call(
        functools.partial(kernel, chunk),
        out_shape=(
            pltpu.VMEM((1, rows, width), jnp.bfloat16),
            pltpu.VMEM((1, width), jnp.float32),
        ),
        in_specs=[outside] * 4,
        out_specs=(vmem, vmem),
        scratch_shapes=[
            pltpu.VMEM((slots, sections, width), jnp.bfloat16),
            pltpu.VMEM((sections, padded, width), jnp.bfloat16),
            pltpu.VMEM((sections, padded, width), jnp.bfloat16),
            pltpu.VMEM((sections, max(odd, 1), width), jnp.float32),
            pltpu.VMEM((sections, max(odd, 1), width), jnp.float32),
            pltpu.VMEM((1, rows), jnp.int32),
            pltpu.VMEM((1, width), jnp.float32),
            pltpu.VMEM((rows, width), jnp.bfloat16),
            pltpu.VMEM((rows, width), jnp.float32),
            pltpu.VMEM((sections, rows, padded), jnp.bfloat16),
            pltpu.VMEM((4, rows, LANES), jnp.float32),
            pltpu.VMEM((n_mp, rows, LANES), jnp.float32),
            pltpu.VMEM((4, rows, LANES), jnp.float32),
            pltpu.VMEM((8, width), jnp.float32),
            pltpu.VMEM((n_dp, 1, width), jnp.float32),
            dma((chunks,)),
            dma((chunks, sections)),
            dma((chunks, sections)),
            dma(()),
            dma((sections,)),
            dma((sections,)),
            dma(()),
            dma(()),
            dma(()),
            dma((n_mp,)),
            dma((n_mp,)),
            dma((n_dp,)),
            dma((n_dp,)),
        ],
        compiler_params=pltpu.CompilerParams(
            collective_id=0, has_side_effects=True, vmem_limit_bytes=56 * 1024 * 1024
        ),
        cost_estimate=pl.CostEstimate(
            flops=2 * rows * sections * slots * width,
            bytes_accessed=2 * width * (sections * slots + 2 * rows),
            transcendentals=0,
        ),
    )(jnp.transpose(held[0], (1, 0, 2)), evict_map.reshape(1, rows), cotangent, gain)


def solution(mesh):
    placed = (
        P("section", None, "dp", "mp"),
        P("section", "dp", None),
        P("section", "dp", "mp"),
        P("section", "mp"),
    )
    return jax.shard_map(
        local,
        mesh=mesh,
        in_specs=placed,
        out_specs=(P("section", "dp", "mp"), P("section", "mp")),
        check_vma=False,
    )
```

```python
import functools

import jax
import jax.numpy as jnp
from jax import lax
from jax.experimental import pallas as pl
from jax.experimental.pallas import tpu as pltpu
from jax.sharding import PartitionSpec as P

MODEL_WIDTH = 12288
LANES = 128
BLOCK = 32
MESH = pl.DeviceIdType.MESH


def kernel(
    chunk, held, holders_hbm, cot_hbm, gain_hbm, dx, gg_out,
    mixed, outbox, recv, odd_out, odd_in, holders, gain, cot, xf, place, part, stats, coef, gsum, gpart,
    held_sem, send_sem, recv_sem, odd_held_sem, odd_send, odd_recv, holders_sem, gain_sem, cot_sem,
    mp_send, mp_recv, dp_send, dp_recv,
):
    slots, sections, width = held.shape
    padded = recv.shape[1]
    main = min(slots, padded)
    odd = slots - main
    rows = cot.shape[0]
    chunks = width // chunk
    blocks = rows // BLOCK
    tiles = chunk // LANES
    n_mp, n_dp = stats.shape[0], gpart.shape[0]
    me = lax.axis_index("section")
    my_mp = lax.axis_index("mp")
    my_dp = lax.axis_index("dp")

    barrier = pltpu.get_barrier_semaphore()
    for axis, mine, size in (("section", me, sections), ("mp", my_mp, n_mp), ("dp", my_dp, n_dp)):
        def greet(i, _, axis=axis, mine=mine, size=size):
            pl.semaphore_signal(
                barrier, inc=1, device_id={axis: lax.rem(mine + i, size)}, device_id_type=MESH
            )
            return 0
        lax.fori_loop(1, size, greet, 0)

    def columns(c):
        return pl.ds(pl.multiple_of(c * chunk, chunk), chunk)

    def fetch(c):
        return pltpu.make_async_copy(
            held.at[0:main, :, columns(c)], mixed.at[0:main, :, columns(c)], held_sem.at[c]
        )
    def start_fetch(c, _):
        fetch(c).start()
        return 0
    lax.fori_loop(0, chunks, start_fetch, 0)
    if odd:
        odd_fetch = pltpu.make_async_copy(
            held.at[main:slots], mixed.at[main:slots], odd_held_sem
        )
        odd_fetch.start()
    cot_copy = pltpu.make_async_copy(cot_hbm.at[0], cot, cot_sem)
    cot_copy.start()
    holders_copy = pltpu.make_async_copy(holders_hbm, holders, holders_sem)
    holders_copy.start()
    gain_copy = pltpu.make_async_copy(gain_hbm, gain, gain_sem)
    gain_copy.start()

    here = lax.broadcasted_iota(jnp.int32, (padded, main * sections), 0)
    there = lax.broadcasted_iota(jnp.int32, (padded, main * sections), 1)
    by_owner = jnp.concatenate(
        [jnp.where(here * sections + s == there, 1.0, 0.0) for s in range(sections)], axis=0
    ).astype(jnp.bfloat16)

    def outgoing(c, i):
        other = lax.rem(me + i, sections)
        return pltpu.make_async_remote_copy(
            src_ref=outbox.at[other, :, columns(c)],
            dst_ref=recv.at[me, :, columns(c)],
            send_sem=send_sem.at[c, i],
            recv_sem=recv_sem.at[c, me],
            device_id={"section": other},
            device_id_type=MESH,
        )

    def incoming(c, i):
        other = lax.rem(me + i, sections)
        return pltpu.make_async_remote_copy(
            src_ref=outbox.at[other, :, columns(c)],
            dst_ref=recv.at[other, :, columns(c)],
            send_sem=send_sem.at[c, i],
            recv_sem=recv_sem.at[c, other],
            device_id={"section": other},
            device_id_type=MESH,
        )

    def odd_copy(i, arriving):
        other = lax.rem(me + i, sections)
        origin = other if arriving else me
        return pltpu.make_async_remote_copy(
            src_ref=odd_out.at[other],
            dst_ref=odd_in.at[origin],
            send_sem=odd_send.at[i],
            recv_sem=odd_recv.at[origin],
            device_id={"section": other},
            device_id_type=MESH,
        )

    def send(c, _):
        fetch(c).wait()
        cols = columns(c)
        rows_by_slot = mixed[0:main, :, cols].reshape(main * sections, chunk)
        sorted_rows = jnp.dot(
            by_owner, rows_by_slot, preferred_element_type=jnp.float32
        ).astype(jnp.bfloat16)
        for s in range(sections):
            outbox[s, :, cols] = sorted_rows[s * padded:(s + 1) * padded]

        def one(i, _):
            outgoing(c, jnp.where(2 * me < sections, sections - i, i)).start()
            return 0
        lax.fori_loop(1, sections, one, 0)
        recv[me, :, cols] = outbox[me, :, cols]
        return 0

    pl.semaphore_wait(barrier, sections + n_mp + n_dp - 3)
    send(0, 0)
    if odd:
        odd_fetch.wait()
        for k in range(odd):
            last = mixed[main + k].astype(jnp.float32)
            for s in range(sections):
                odd_out[s, k:k + 1, :] = last[s:s + 1]

        def send_odd(i, _):
            odd_copy(i, False).start()
            return 0
        lax.fori_loop(1, sections, send_odd, 0)
        odd_in[me] = odd_out[me]
    lax.fori_loop(1, chunks, send, 0)

    holders_copy.wait()
    across = lax.broadcasted_iota(jnp.int32, (rows, rows), 1)
    down = lax.broadcasted_iota(jnp.int32, (rows, rows), 0)
    named = holders[...].astype(jnp.float32)
    holder = jnp.sum(jnp.where(across == down, named, 0.0), axis=1, keepdims=True)
    lane = lax.broadcasted_iota(jnp.int32, (rows, LANES), 1)
    onehot = jnp.where(holder == lane.astype(jnp.float32), 1.0, 0.0)
    upto = jnp.where(down >= across, 1.0, 0.0).astype(jnp.bfloat16)
    count = jnp.dot(upto, onehot.astype(jnp.bfloat16), preferred_element_type=jnp.float32)
    slot = jnp.sum(count * onehot, axis=1, keepdims=True) - 1.0
    number = lax.broadcasted_iota(jnp.int32, (rows, padded), 1).astype(jnp.float32)
    for s in range(sections):
        place[s] = jnp.where(
            jnp.logical_and(holder == float(s), slot == number), 1.0, 0.0
        ).astype(jnp.bfloat16)
    number = lax.broadcasted_iota(jnp.int32, (rows, sections), 1).astype(jnp.float32)
    odd_place = [
        jnp.where(
            jnp.logical_and(holder == number, slot == float(main + k)), 1.0, 0.0
        ).astype(jnp.bfloat16)
        for k in range(odd)
    ]
    part[...] = jnp.zeros_like(part)
    gsum[...] = jnp.zeros_like(gsum)

    cot_copy.wait()
    gain_copy.wait()
    if odd:
        def odd_arrive(i, _):
            odd_copy(i, True).wait_recv()
            return 0
        lax.fori_loop(1, sections, odd_arrive, 0)

    def work(c, _):
        def arrive(i, _):
            incoming(c, i).wait_recv()
            return 0
        lax.fori_loop(1, sections, arrive, 0)
        cols = columns(c)
        total = jnp.dot(place[0], recv[0, :, cols], preferred_element_type=jnp.float32)
        for s in range(1, sections):
            total += jnp.dot(place[s], recv[s, :, cols], preferred_element_type=jnp.float32)
        for k in range(odd):
            extra = jnp.concatenate([odd_in[s, k:k + 1, cols] for s in range(sections)], axis=0)
            total += jnp.dot(
                odd_place[k], extra.astype(jnp.bfloat16), preferred_element_type=jnp.float32
            )
        xf[:, cols] = total

        def block(b, _):
            rws = pl.ds(pl.multiple_of(b * BLOCK, BLOCK), BLOCK)
            sums = [part[k, rws] for k in range(4)]
            for t in range(tiles):
                at = pl.ds(pl.multiple_of(c * chunk + t * LANES, LANES), LANES)
                x = xf[rws, at]
                g = gain[:, at] * cot[rws, at].astype(jnp.float32)
                sums = [sums[0] + x, sums[1] + x * x, sums[2] + g, sums[3] + g * x]
            for k in range(4):
                part[k, rws] = sums[k]
            return 0
        lax.fori_loop(0, blocks, block, 0)
        return 0
    lax.fori_loop(0, chunks, work, 0)

    lane = lax.broadcasted_iota(jnp.int32, (rows, LANES), 1)
    packed = jnp.zeros((rows, LANES), jnp.float32)
    for k in range(4):
        packed = jnp.where(lane == k, jnp.sum(part[k], axis=1, keepdims=True), packed)
    stats[my_mp] = packed

    def exchange(ref, axis, mine, size, sends, recvs, arriving):
        def copy(i):
            other = lax.rem(mine + i, size)
            return pltpu.make_async_remote_copy(
                src_ref=ref.at[mine],
                dst_ref=ref.at[other if arriving else mine],
                send_sem=sends.at[i],
                recv_sem=recvs.at[other if arriving else mine],
                device_id={axis: other},
                device_id_type=MESH,
            )
        return copy

    mp_out = exchange(stats, "mp", my_mp, n_mp, mp_send, mp_recv, False)
    mp_in = exchange(stats, "mp", my_mp, n_mp, mp_send, mp_recv, True)
    dp_out = exchange(gpart, "dp", my_dp, n_dp, dp_send, dp_recv, False)
    dp_in = exchange(gpart, "dp", my_dp, n_dp, dp_send, dp_recv, True)
    for i in range(1, n_mp):
        mp_out(i).start()
    for i in range(1, n_mp):
        mp_in(i).wait_recv()

    both = stats[0]
    for i in range(1, n_mp):
        both += stats[i]
    mean = both[:, 0:1] / MODEL_WIDTH
    rstd = 1.0 / jnp.sqrt(both[:, 1:2] / MODEL_WIDTH - mean * mean + 1e-05)
    m1 = both[:, 2:3] / MODEL_WIDTH
    m2 = rstd * (both[:, 3:4] / MODEL_WIDTH - mean * m1)
    for k, value in enumerate((mean, rstd, -rstd * rstd * m2, -rstd * m1)):
        coef[k] = jnp.broadcast_to(value, (rows, LANES))

    def gain_block(b, _):
        rws = pl.ds(pl.multiple_of(b * BLOCK, BLOCK), BLOCK)
        mean, rstd = coef[0, rws], coef[1, rws]

        def tile(t, _):
            at = pl.ds(pl.multiple_of(t * LANES, LANES), LANES)
            p = cot[rws, at].astype(jnp.float32) * ((xf[rws, at] - mean) * rstd)
            q = p[0:8]
            for j in range(8, BLOCK, 8):
                q += p[j:j + 8]
            gsum[:, at] += q
            return 0
        return lax.fori_loop(0, width // LANES, tile, 0, unroll=8)
    lax.fori_loop(0, blocks, gain_block, 0)
    gpart[my_dp] = jnp.sum(gsum[...], axis=0, keepdims=True)
    for i in range(1, n_dp):
        dp_out(i).start()

    def grad_block(b, _):
        rws = pl.ds(pl.multiple_of(b * BLOCK, BLOCK), BLOCK)
        mean, rstd, slope, shift = (coef[k, rws] for k in range(4))

        def tile(t, _):
            at = pl.ds(pl.multiple_of(t * LANES, LANES), LANES)
            g = gain[:, at] * cot[rws, at].astype(jnp.float32)
            dx[0, rws, at] = (rstd * g + shift + (xf[rws, at] - mean) * slope).astype(jnp.bfloat16)
            return 0
        lax.fori_loop(0, width // LANES, tile, 0, unroll=8)
        return 0
    lax.fori_loop(0, blocks, grad_block, 0)

    for i in range(1, n_dp):
        dp_in(i).wait_recv()
    total = gpart[0]
    for i in range(1, n_dp):
        total += gpart[i]
    gg_out[...] = total

    for i in range(1, n_dp):
        dp_out(i).wait_send()
    for i in range(1, n_mp):
        mp_out(i).wait_send()

    def sent(c, _):
        def one(i, _):
            outgoing(c, i).wait_send()
            return 0
        return lax.fori_loop(1, sections, one, 0)
    lax.fori_loop(0, chunks, sent, 0)
    if odd:
        def odd_sent(i, _):
            odd_copy(i, False).wait_send()
            return 0
        lax.fori_loop(1, sections, odd_sent, 0)


def local(held, evict_map, cotangent, gain):
    sections, n_mp, n_dp = (lax.axis_size(a) for a in ("section", "mp", "dp"))
    _, _, slots, width = held.shape
    rows = cotangent.shape[1]
    chunk = 512 if width % 512 == 0 else width
    chunks = width // chunk
    odd = slots % 8 if slots > 8 and slots % 8 <= 3 else 0
    padded = -(-(slots - odd) // 8) * 8
    outside = pl.BlockSpec(memory_space=pltpu.HBM)
    vmem = pl.BlockSpec(memory_space=pltpu.VMEM)
    dma = pltpu.SemaphoreType.DMA
    return pl.pallas_call(
        functools.partial(kernel, chunk),
        out_shape=(
            pltpu.VMEM((1, rows, width), jnp.bfloat16),
            pltpu.VMEM((1, width), jnp.float32),
        ),
        in_specs=[outside] * 4,
        out_specs=(vmem, vmem),
        scratch_shapes=[
            pltpu.VMEM((slots, sections, width), jnp.bfloat16),
            pltpu.VMEM((sections, padded, width), jnp.bfloat16),
            pltpu.VMEM((sections, padded, width), jnp.bfloat16),
            pltpu.VMEM((sections, max(odd, 1), width), jnp.float32),
            pltpu.VMEM((sections, max(odd, 1), width), jnp.float32),
            pltpu.VMEM((1, rows), jnp.int32),
            pltpu.VMEM((1, width), jnp.float32),
            pltpu.VMEM((rows, width), jnp.bfloat16),
            pltpu.VMEM((rows, width), jnp.float32),
            pltpu.VMEM((sections, rows, padded), jnp.bfloat16),
            pltpu.VMEM((4, rows, LANES), jnp.float32),
            pltpu.VMEM((n_mp, rows, LANES), jnp.float32),
            pltpu.VMEM((4, rows, LANES), jnp.float32),
            pltpu.VMEM((8, width), jnp.float32),
            pltpu.VMEM((n_dp, 1, width), jnp.float32),
            dma((chunks,)),
            dma((chunks, sections)),
            dma((chunks, sections)),
            dma(()),
            dma((sections,)),
            dma((sections,)),
            dma(()),
            dma(()),
            dma(()),
            dma((n_mp,)),
            dma((n_mp,)),
            dma((n_dp,)),
            dma((n_dp,)),
        ],
        compiler_params=pltpu.CompilerParams(
            collective_id=0, has_side_effects=True, vmem_limit_bytes=56 * 1024 * 1024
        ),
        cost_estimate=pl.CostEstimate(
            flops=2 * rows * sections * slots * width,
            bytes_accessed=2 * width * (sections * slots + 2 * rows),
            transcendentals=0,
        ),
    )(jnp.transpose(held[0], (1, 0, 2)), evict_map.reshape(1, rows), cotangent, gain)


def solution(mesh):
    placed = (
        P("section", None, "dp", "mp"),
        P("section", "dp", None),
        P("section", "dp", "mp"),
        P("section", "mp"),
    )
    return jax.shard_map(
        local,
        mesh=mesh,
        in_specs=placed,
        out_specs=(P("section", "dp", "mp"), P("section", "mp")),
        check_vma=False,
    )
```

```python
import functools

import jax
import jax.numpy as jnp
from jax import lax
from jax.experimental import pallas as pl
from jax.experimental.pallas import tpu as pltpu
from jax.sharding import PartitionSpec as P

MODEL_WIDTH = 12288
LANES = 128
BLOCK = 32
MESH = pl.DeviceIdType.MESH


def kernel(
    chunk, held, holders_hbm, cot_hbm, gain_hbm, dx, gg_out,
    mixed, outbox, recv, odd_out, odd_in, holders, gain, cot, xf, place, part, stats, coef, gsum, gpart,
    held_sem, send_sem, recv_sem, odd_held_sem, odd_send, odd_recv, holders_sem, gain_sem, cot_sem,
    mp_send, mp_recv, dp_send, dp_recv,
):
    slots, sections, width = held.shape
    padded = recv.shape[1]
    main = min(slots, padded)
    odd = slots - main
    rows = cot.shape[0]
    chunks = width // chunk
    blocks = rows // BLOCK
    tiles = chunk // LANES
    n_mp, n_dp = stats.shape[0], gpart.shape[0]
    me = lax.axis_index("section")
    my_mp = lax.axis_index("mp")
    my_dp = lax.axis_index("dp")

    barrier = pltpu.get_barrier_semaphore()
    for axis, mine, size in (("section", me, sections), ("mp", my_mp, n_mp), ("dp", my_dp, n_dp)):
        def greet(i, _, axis=axis, mine=mine, size=size):
            pl.semaphore_signal(
                barrier, inc=1, device_id={axis: lax.rem(mine + i, size)}, device_id_type=MESH
            )
            return 0
        lax.fori_loop(1, size, greet, 0)

    def columns(c):
        return pl.ds(pl.multiple_of(c * chunk, chunk), chunk)

    def fetch(c):
        return pltpu.make_async_copy(
            held.at[0:main, :, columns(c)], mixed.at[0:main, :, columns(c)], held_sem.at[c]
        )
    def start_fetch(c, _):
        fetch(c).start()
        return 0
    lax.fori_loop(0, chunks, start_fetch, 0)
    if odd:
        odd_fetch = pltpu.make_async_copy(
            held.at[main:slots], mixed.at[main:slots], odd_held_sem
        )
        odd_fetch.start()
    cot_copy = pltpu.make_async_copy(cot_hbm.at[0], cot, cot_sem)
    cot_copy.start()
    holders_copy = pltpu.make_async_copy(holders_hbm, holders, holders_sem)
    holders_copy.start()
    gain_copy = pltpu.make_async_copy(gain_hbm, gain, gain_sem)
    gain_copy.start()

    here = lax.broadcasted_iota(jnp.int32, (padded, main * sections), 0)
    there = lax.broadcasted_iota(jnp.int32, (padded, main * sections), 1)
    by_owner = jnp.concatenate(
        [jnp.where(here * sections + s == there, 1.0, 0.0) for s in range(sections)], axis=0
    ).astype(jnp.bfloat16)

    def outgoing(c, i):
        other = lax.rem(me + i, sections)
        return pltpu.make_async_remote_copy(
            src_ref=outbox.at[other, :, columns(c)],
            dst_ref=recv.at[me, :, columns(c)],
            send_sem=send_sem.at[c, i],
            recv_sem=recv_sem.at[c, me],
            device_id={"section": other},
            device_id_type=MESH,
        )

    def incoming(c, i):
        other = lax.rem(me + i, sections)
        return pltpu.make_async_remote_copy(
            src_ref=outbox.at[other, :, columns(c)],
            dst_ref=recv.at[other, :, columns(c)],
            send_sem=send_sem.at[c, i],
            recv_sem=recv_sem.at[c, other],
            device_id={"section": other},
            device_id_type=MESH,
        )

    def odd_copy(i, arriving):
        other = lax.rem(me + i, sections)
        origin = other if arriving else me
        return pltpu.make_async_remote_copy(
            src_ref=odd_out.at[other],
            dst_ref=odd_in.at[origin],
            send_sem=odd_send.at[i],
            recv_sem=odd_recv.at[origin],
            device_id={"section": other},
            device_id_type=MESH,
        )

    def send(c, _):
        fetch(c).wait()
        cols = columns(c)
        rows_by_slot = mixed[0:main, :, cols].reshape(main * sections, chunk)
        sorted_rows = jnp.dot(
            by_owner, rows_by_slot, preferred_element_type=jnp.float32
        ).astype(jnp.bfloat16)
        for s in range(sections):
            outbox[s, :, cols] = sorted_rows[s * padded:(s + 1) * padded]

        def one(i, _):
            outgoing(c, jnp.where(2 * me < sections, sections - i, i)).start()
            return 0
        lax.fori_loop(1, sections, one, 0)
        recv[me, :, cols] = outbox[me, :, cols]
        return 0

    pl.semaphore_wait(barrier, sections + n_mp + n_dp - 3)
    send(0, 0)
    if odd:
        odd_fetch.wait()
        for k in range(odd):
            last = mixed[main + k].astype(jnp.float32)
            for s in range(sections):
                odd_out[s, k:k + 1, :] = last[s:s + 1]

        def send_odd(i, _):
            odd_copy(i, False).start()
            return 0
        lax.fori_loop(1, sections, send_odd, 0)
        odd_in[me] = odd_out[me]
    lax.fori_loop(1, chunks, send, 0)

    holders_copy.wait()
    across = lax.broadcasted_iota(jnp.int32, (rows, rows), 1)
    down = lax.broadcasted_iota(jnp.int32, (rows, rows), 0)
    named = holders[...].astype(jnp.float32)
    holder = jnp.sum(jnp.where(across == down, named, 0.0), axis=1, keepdims=True)
    lane = lax.broadcasted_iota(jnp.int32, (rows, LANES), 1)
    onehot = jnp.where(holder == lane.astype(jnp.float32), 1.0, 0.0)
    upto = jnp.where(down >= across, 1.0, 0.0).astype(jnp.bfloat16)
    count = jnp.dot(upto, onehot.astype(jnp.bfloat16), preferred_element_type=jnp.float32)
    slot = jnp.sum(count * onehot, axis=1, keepdims=True) - 1.0
    number = lax.broadcasted_iota(jnp.int32, (rows, padded), 1).astype(jnp.float32)
    for s in range(sections):
        place[s] = jnp.where(
            jnp.logical_and(holder == float(s), slot == number), 1.0, 0.0
        ).astype(jnp.bfloat16)
    number = lax.broadcasted_iota(jnp.int32, (rows, sections), 1).astype(jnp.float32)
    odd_place = [
        jnp.where(
            jnp.logical_and(holder == number, slot == float(main + k)), 1.0, 0.0
        ).astype(jnp.bfloat16)
        for k in range(odd)
    ]
    part[...] = jnp.zeros_like(part)
    gsum[...] = jnp.zeros_like(gsum)

    cot_copy.wait()
    gain_copy.wait()
    if odd:
        def odd_arrive(i, _):
            odd_copy(i, True).wait_recv()
            return 0
        lax.fori_loop(1, sections, odd_arrive, 0)

    def work(c, _):
        def arrive(i, _):
            incoming(c, i).wait_recv()
            return 0
        lax.fori_loop(1, sections, arrive, 0)
        cols = columns(c)
        total = jnp.dot(place[0], recv[0, :, cols], preferred_element_type=jnp.float32)
        for s in range(1, sections):
            total += jnp.dot(place[s], recv[s, :, cols], preferred_element_type=jnp.float32)
        for k in range(odd):
            extra = jnp.concatenate([odd_in[s, k:k + 1, cols] for s in range(sections)], axis=0)
            total += jnp.dot(
                odd_place[k], extra.astype(jnp.bfloat16), preferred_element_type=jnp.float32
            )
        xf[:, cols] = total

        def block(b, _):
            rws = pl.ds(pl.multiple_of(b * BLOCK, BLOCK), BLOCK)
            sums = [part[k, rws] for k in range(4)]
            for t in range(tiles):
                at = pl.ds(pl.multiple_of(c * chunk + t * LANES, LANES), LANES)
                x = xf[rws, at]
                g = gain[:, at] * cot[rws, at].astype(jnp.float32)
                sums = [sums[0] + x, sums[1] + x * x, sums[2] + g, sums[3] + g * x]
            for k in range(4):
                part[k, rws] = sums[k]
            return 0
        lax.fori_loop(0, blocks, block, 0)
        return 0
    lax.fori_loop(0, chunks, work, 0)

    lane = lax.broadcasted_iota(jnp.int32, (rows, LANES), 1)
    packed = jnp.zeros((rows, LANES), jnp.float32)
    for k in range(4):
        packed = jnp.where(lane == k, jnp.sum(part[k], axis=1, keepdims=True), packed)
    stats[my_mp] = packed

    def exchange(ref, axis, mine, size, sends, recvs, arriving):
        def copy(i):
            other = lax.rem(mine + i, size)
            return pltpu.make_async_remote_copy(
                src_ref=ref.at[mine],
                dst_ref=ref.at[other if arriving else mine],
                send_sem=sends.at[i],
                recv_sem=recvs.at[other if arriving else mine],
                device_id={axis: other},
                device_id_type=MESH,
            )
        return copy

    mp_out = exchange(stats, "mp", my_mp, n_mp, mp_send, mp_recv, False)
    mp_in = exchange(stats, "mp", my_mp, n_mp, mp_send, mp_recv, True)
    dp_out = exchange(gpart, "dp", my_dp, n_dp, dp_send, dp_recv, False)
    dp_in = exchange(gpart, "dp", my_dp, n_dp, dp_send, dp_recv, True)
    for i in range(1, n_mp):
        mp_out(i).start()
    for i in range(1, n_mp):
        mp_in(i).wait_recv()

    both = stats[0]
    for i in range(1, n_mp):
        both += stats[i]
    mean = both[:, 0:1] / MODEL_WIDTH
    rstd = 1.0 / jnp.sqrt(both[:, 1:2] / MODEL_WIDTH - mean * mean + 1e-05)
    m1 = both[:, 2:3] / MODEL_WIDTH
    m2 = rstd * (both[:, 3:4] / MODEL_WIDTH - mean * m1)
    for k, value in enumerate((mean, rstd, -rstd * rstd * m2, -rstd * m1)):
        coef[k] = jnp.broadcast_to(value, (rows, LANES))

    def gain_block(b, _):
        rws = pl.ds(pl.multiple_of(b * BLOCK, BLOCK), BLOCK)
        mean, rstd = coef[0, rws], coef[1, rws]

        def tile(t, _):
            at = pl.ds(pl.multiple_of(t * LANES, LANES), LANES)
            p = cot[rws, at].astype(jnp.float32) * ((xf[rws, at] - mean) * rstd)
            q = p[0:8]
            for j in range(8, BLOCK, 8):
                q += p[j:j + 8]
            gsum[:, at] += q
            return 0
        return lax.fori_loop(0, width // LANES, tile, 0, unroll=8)
    lax.fori_loop(0, blocks, gain_block, 0)
    gpart[my_dp] = jnp.sum(gsum[...], axis=0, keepdims=True)
    for i in range(1, n_dp):
        dp_out(i).start()

    def grad_block(b, _):
        rws = pl.ds(pl.multiple_of(b * BLOCK, BLOCK), BLOCK)
        mean, rstd, slope, shift = (coef[k, rws] for k in range(4))

        def tile(t, _):
            at = pl.ds(pl.multiple_of(t * LANES, LANES), LANES)
            g = gain[:, at] * cot[rws, at].astype(jnp.float32)
            dx[0, rws, at] = (rstd * g + shift + (xf[rws, at] - mean) * slope).astype(jnp.bfloat16)
            return 0
        lax.fori_loop(0, width // LANES, tile, 0, unroll=8)
        return 0
    lax.fori_loop(0, blocks, grad_block, 0)

    for i in range(1, n_dp):
        dp_in(i).wait_recv()
    total = gpart[0]
    for i in range(1, n_dp):
        total += gpart[i]
    gg_out[...] = total

    for i in range(1, n_dp):
        dp_out(i).wait_send()
    for i in range(1, n_mp):
        mp_out(i).wait_send()

    def sent(c, _):
        def one(i, _):
            outgoing(c, i).wait_send()
            return 0
        return lax.fori_loop(1, sections, one, 0)
    lax.fori_loop(0, chunks, sent, 0)
    if odd:
        def odd_sent(i, _):
            odd_copy(i, False).wait_send()
            return 0
        lax.fori_loop(1, sections, odd_sent, 0)


def local(held, evict_map, cotangent, gain):
    sections, n_mp, n_dp = (lax.axis_size(a) for a in ("section", "mp", "dp"))
    _, _, slots, width = held.shape
    rows = cotangent.shape[1]
    chunk = 1024 if width % 1024 == 0 else width
    chunks = width // chunk
    odd = slots % 8 if slots > 8 and slots % 8 <= 3 else 0
    padded = -(-(slots - odd) // 8) * 8
    outside = pl.BlockSpec(memory_space=pltpu.HBM)
    vmem = pl.BlockSpec(memory_space=pltpu.VMEM)
    dma = pltpu.SemaphoreType.DMA
    return pl.pallas_call(
        functools.partial(kernel, chunk),
        out_shape=(
            pltpu.VMEM((1, rows, width), jnp.bfloat16),
            pltpu.VMEM((1, width), jnp.float32),
        ),
        in_specs=[outside] * 4,
        out_specs=(vmem, vmem),
        scratch_shapes=[
            pltpu.VMEM((slots, sections, width), jnp.bfloat16),
            pltpu.VMEM((sections, padded, width), jnp.bfloat16),
            pltpu.VMEM((sections, padded, width), jnp.bfloat16),
            pltpu.VMEM((sections, max(odd, 1), width), jnp.float32),
            pltpu.VMEM((sections, max(odd, 1), width), jnp.float32),
            pltpu.VMEM((1, rows), jnp.int32),
            pltpu.VMEM((1, width), jnp.float32),
            pltpu.VMEM((rows, width), jnp.bfloat16),
            pltpu.VMEM((rows, width), jnp.float32),
            pltpu.VMEM((sections, rows, padded), jnp.bfloat16),
            pltpu.VMEM((4, rows, LANES), jnp.float32),
            pltpu.VMEM((n_mp, rows, LANES), jnp.float32),
            pltpu.VMEM((4, rows, LANES), jnp.float32),
            pltpu.VMEM((8, width), jnp.float32),
            pltpu.VMEM((n_dp, 1, width), jnp.float32),
            dma((chunks,)),
            dma((chunks, sections)),
            dma((chunks, sections)),
            dma(()),
            dma((sections,)),
            dma((sections,)),
            dma(()),
            dma(()),
            dma(()),
            dma((n_mp,)),
            dma((n_mp,)),
            dma((n_dp,)),
            dma((n_dp,)),
        ],
        compiler_params=pltpu.CompilerParams(
            collective_id=0, has_side_effects=True, vmem_limit_bytes=56 * 1024 * 1024
        ),
        cost_estimate=pl.CostEstimate(
            flops=2 * rows * sections * slots * width,
            bytes_accessed=2 * width * (sections * slots + 2 * rows),
            transcendentals=0,
        ),
    )(jnp.transpose(held[0], (1, 0, 2)), evict_map.reshape(1, rows), cotangent, gain)


def solution(mesh):
    placed = (
        P("section", None, "dp", "mp"),
        P("section", "dp", None),
        P("section", "dp", "mp"),
        P("section", "mp"),
    )
    return jax.shard_map(
        local,
        mesh=mesh,
        in_specs=placed,
        out_specs=(P("section", "dp", "mp"), P("section", "mp")),
        check_vma=False,
    )
```
